32 devices in a mesh: leaf: 2 (over y), row: 2 (over x), col: 8 (over z, core).
Axes of the slice: x: 2, y: 2, z: 4, core: 2. Of those that a mesh axis runs over, the one named last changes fastest.
Arguments:
- front_window: float32 [49152, 2048], P(('leaf', 'row'), 'col'), parts along dimension 0, may hold values from -8 to 785
- children: float32 [65536, 2048], P(('leaf', 'row', 'col')), parts along dimension 0, may hold values from -1 to 1
- row_map: int32 [4, 128], P('leaf'), parts along dimension 0, may hold values from 0 to 191, as said below
- col_map: int32 [4, 16], P('leaf'), parts along dimension 0, may hold values from 0 to 15, as said below
Outputs:
- factored: float32 [49152, 2048], P(('leaf', 'row'), 'col'), parts along dimension 0
The draws below stay inside these ranges and needn't reach their ends.
There are 2 independent parts, one for each index of `leaf`. The reference program is written for one: setup_inputs(seed, part) draws one part's arguments, and reference() takes and returns one part's arrays. A program takes and returns all parts, laid end to end along the dimension named above; each array names one. Nothing has to cross between parts.
Inputs may be any that keep to these rules, and one draw needn't show every extreme that they name: `row_map`: for each sibling, its entries are distinct; each aligned run of 128 of its row blocks names exactly 64 blocks in each range of 96 consecutive parent blocks. `col_map`: each sibling's row is a permutation of the 16 window blocks.
All inputs are finite; a program needn't handle non-finite values.
Results may differ from the reference program's by a relative error of at most 0.000088.
Values sent between devices are 32-bit elements; how exact they have to be, the bound alone decides.
A program may use at most 192 MiB of HBM per device.

```python
import jax
import jax.numpy as jnp
from jax import lax

BLK = 128
P_SIZE = 24576
C = 16384
PANEL = 256
W = 2048
CB = 128
WB = 16
PBD = 96
QB = 128
CAPB = 64
N_ROW = 2


def draw_front_window(key, part):
    row_index = lax.broadcasted_iota(jnp.int32, (P_SIZE, W), 0)
    col_index = lax.broadcasted_iota(jnp.int32, (P_SIZE, W), 1)
    values = jax.random.uniform(key, (P_SIZE, W), jnp.float32, -1.0, 1.0)
    values = jnp.where((col_index < PANEL) & (row_index >= PANEL), 8.0 * values, values)
    values = values + jnp.where(row_index == col_index, 3.0 * PANEL + 16.0, 0.0)
    return values.astype(jnp.float32)


def pick_offsets(subkey):
    inner = jax.random.permutation(subkey, PBD - 2)[:CB // N_ROW - 2] + 1
    edges = jnp.array([0, PBD - 1], dtype=jnp.int32)
    return jnp.sort(jnp.concatenate([edges, inner.astype(jnp.int32)]))


def draw_row_map(key, part):
    result_rows = []
    for sibling in range(2):
        folded = jax.random.fold_in(key, 11 + sibling)
        first, second = jax.random.split(folded)
        pattern = (jnp.arange(QB, dtype=jnp.int32) // CAPB).astype(jnp.int32)
        quarter_keys = jax.random.split(first, N_ROW // 2)
        owners = jax.vmap(lambda subkey: jax.random.permutation(subkey, pattern))(quarter_keys).reshape(-1)
        onehot = (owners[:, None] == jnp.arange(N_ROW, dtype=jnp.int32)[None, :]).astype(jnp.int32)
        ranks = jnp.sum((jnp.cumsum(onehot, axis=0) - onehot) * onehot, axis=1)
        offsets = jax.vmap(pick_offsets)(jax.random.split(second, N_ROW))
        result_rows.append(owners * PBD + offsets[owners, ranks])
    return jnp.stack(result_rows).astype(jnp.int32)


def draw_col_map(key, part):
    first = jax.random.permutation(jax.random.fold_in(key, 21), WB)
    second = jax.random.permutation(jax.random.fold_in(key, 22), WB)
    return jnp.stack([first, second]).astype(jnp.int32)


def shard_levels(rng, shape, cuts, smallest, high):
    loudness = 1.0
    for position, blocks in cuts:
        heights = jax.random.uniform(jax.random.fold_in(jax.random.fold_in(rng, 6), position), (blocks,), jnp.float32, smallest / len(cuts), high / len(cuts))
        loudness = loudness * jnp.repeat(jnp.exp(heights), shape[position] // blocks).reshape((-1,) + (1,) * (len(shape) - 1 - position))
    return loudness


def setup_inputs(seed: int = 0, part: int = 0) -> dict:
    arg_keys = jax.random.split(jax.random.key(seed), 5)
    part_splits = jax.random.split(jax.random.fold_in(arg_keys[4], part), 5)
    return {
        "front_window": draw_front_window(jax.random.fold_in(jax.random.fold_in(arg_keys[4], part), 71), part),
        "children": jnp.clip(jax.random.uniform(part_splits[1], (2 * C, W), jnp.float32, -1.0, 1.0) * shard_levels(part_splits[1], (2 * C, W), ((0, 16),), -0.4, 0.0), -1.0, 1.0),
        "row_map": draw_row_map(jax.random.fold_in(jax.random.fold_in(arg_keys[4], part), 71), part),
        "col_map": draw_col_map(jax.random.fold_in(jax.random.fold_in(arg_keys[4], part), 71), part),
    }


def reference(front_window, children, row_map, col_map):
    blocks = front_window.reshape(P_SIZE // BLK, BLK, W // BLK, BLK)
    for sibling in range(2):
        part_rows = children[sibling * C:(sibling + 1) * C].reshape(C // BLK, BLK, W // BLK, BLK)
        placed = jnp.zeros_like(part_rows).at[:, :, col_map[sibling], :].set(part_rows)
        blocks = blocks.at[row_map[sibling]].add(placed)
    assembled = blocks.reshape(P_SIZE, W)
    diagonal_block = assembled[:PANEL, :PANEL]
    factor = jnp.linalg.cholesky(diagonal_block)
    inverse = jax.scipy.linalg.solve_triangular(factor, jnp.eye(PANEL, dtype=factor.dtype), lower=True)
    solved = jnp.dot(assembled[PANEL:, :PANEL], inverse.T, precision=lax.Precision.HIGHEST)
    trailing = assembled[PANEL:, PANEL:] - jnp.dot(solved, solved[:W - PANEL].T, precision=lax.Precision.HIGHEST)
    upper_rows = jnp.concatenate([factor, assembled[:PANEL, PANEL:]], axis=1)
    bottom = jnp.concatenate([solved, trailing], axis=1)
    return jnp.concatenate([upper_rows, bottom], axis=0)
```

```python
import functools

import jax
import jax.numpy as jnp
from jax import lax
from jax.experimental import pallas as pl
from jax.experimental.pallas import tpu as pltpu
from jax.sharding import PartitionSpec as P

BLK = 128
PANEL = 256
PB = PANEL // BLK
NCH = 8
SUB = BLK // NCH
HI = lax.Precision.HIGHEST
MESH = pl.DeviceIdType.MESH
VMEM_LIMIT = 60 * 1024 * 1024


def pack_kernel(index_ref, child_ref, out_ref):
    out_ref[0] = child_ref[...]


def pack(children, inverse_cols, col_count, cols_here):
    child_rows, width = children.shape
    per = cols_here // BLK
    return pl.pallas_call(
        pack_kernel,
        grid_spec=pltpu.PrefetchScalarGridSpec(
            num_scalar_prefetch=1,
            grid=(width // BLK,),
            in_specs=[pl.BlockSpec((child_rows, BLK), lambda k, idx: (0, idx[k]))],
            out_specs=pl.BlockSpec((1, child_rows, BLK), lambda k, idx: (k // per, 0, k % per)),
        ),
        out_shape=jax.ShapeDtypeStruct((col_count, child_rows, cols_here), jnp.float32),
        compiler_params=pltpu.CompilerParams(vmem_limit_bytes=32 * 1024 * 1024),
    )(inverse_cols, children)


def move_kernel(dims, order_ref, place_ref, send_ref, front_ref, asm_ref, panel_ref, match_ref, diag_ref, *scratch):
    C, R, nb, cap, pb = dims
    zin, xout, xin, buf = (scratch[i * NCH:(i + 1) * NCH] for i in range(4))
    zs, zr, zl, xs, xr, fl, ol, ps, pr, pl_sem, ms, mr, ml = scratch[4 * NCH:]
    c = lax.axis_index("col")
    r = lax.axis_index("row")
    even = lax.rem(c, 2) == 0

    def rows(j):
        return pl.ds(j * SUB, SUB)

    def front_copy(j):
        return pltpu.make_async_copy(front_ref.at[:, rows(j), :], buf[j], fl.at[j])

    def own_copy(j):
        return pltpu.make_async_copy(
            send_ref.at[c, :, rows(j), :], zin[j].at[pl.ds(c * nb, nb)], zl.at[j]
        )

    def z_copy(j, dest, source):
        return pltpu.make_async_remote_copy(
            src_ref=send_ref.at[dest, :, rows(j), :],
            dst_ref=zin[j].at[pl.ds(source * nb, nb)],
            send_sem=zs.at[j, dest],
            recv_sem=zr.at[j, source],
            device_id={"col": dest},
            device_id_type=MESH,
        )

    def x_copy(j, o, dest, source):
        return pltpu.make_async_remote_copy(
            src_ref=xout[j].at[o - 1],
            dst_ref=xin[j].at[pl.ds(source * cap, cap)],
            send_sem=xs.at[j, o - 1],
            recv_sem=xr.at[j, source],
            device_id={"row": dest},
            device_id_type=MESH,
        )

    def p_copy(j, source, hop):
        return pltpu.make_async_remote_copy(
            src_ref=source,
            dst_ref=panel_ref.at[:, rows(j), :],
            send_sem=ps.at[j, hop - 1],
            recv_sem=pr.at[j],
            device_id={"col": lax.rem(c + hop, C)},
            device_id_type=MESH,
        )

    def out_copy(j):
        return pltpu.make_async_copy(buf[j], asm_ref.at[:, rows(j), :], ol.at[j])

    def panel_keep(j):
        return pltpu.make_async_copy(buf[j], panel_ref.at[:, rows(j), :], pl_sem.at[j])

    for j in range(NCH):
        own_copy(j).start()
        front_copy(j).start()
        xin[j][R * cap] = jnp.zeros(xin[j].shape[1:], jnp.float32)

    barrier = pltpu.get_barrier_semaphore()
    for d in range(1, C):
        pl.semaphore_signal(barrier, inc=1, device_id={"col": lax.rem(c + d, C)}, device_id_type=MESH)
    for o in range(1, R):
        pl.semaphore_signal(barrier, inc=1, device_id={"row": lax.rem(r + o, R)}, device_id_type=MESH)
    pl.semaphore_wait(barrier, C + R - 2)

    @pl.when(c != 0)
    def _():
        for j in range(NCH):
            z_copy(j, 0, c).start()

    for j in range(NCH):

        @pl.loop(1, C)
        def _(d):
            dest = lax.rem(c + d, C)

            @pl.when(dest != 0)
            def _():
                z_copy(j, dest, c).start()

    def panel_forward(j):
        @pl.when(c != 0)
        def _():
            p_copy(j, panel_ref.at[:, rows(j), :], 1).wait_recv()

            @pl.when(even)
            def _():
                p_copy(j, panel_ref.at[:, rows(j), :], 1).start()

                @pl.when(c + 2 < C)
                def _():
                    p_copy(j, panel_ref.at[:, rows(j), :], 2).start()

    def exchange(j):
        own_copy(j).wait()

        @pl.loop(1, C)
        def _(d):
            source = lax.rem(c + d, C)
            z_copy(j, source, source).wait_recv()

        for o in range(1, R):
            dest = lax.rem(r + o, R)

            @pl.loop(0, cap)
            def _(s):
                xout[j][o - 1, s] = zin[j][order_ref[dest * cap + s]]

            x_copy(j, o, dest, r).start()

        @pl.loop(0, cap)
        def _(s):
            xin[j][r * cap + s] = zin[j][order_ref[r * cap + s]]

    def assemble(j):
        front_copy(j).wait()
        for o in range(1, R):
            source = lax.rem(r + o, R)
            x_copy(j, o, source, source).wait_recv()

        @pl.loop(0, pb)
        def _(p):
            buf[j][p] = buf[j][p] + xin[j][place_ref[p]] + xin[j][place_ref[pb + p]]

        out_copy(j).start()

        @pl.when(c == 0)
        def _():
            panel_keep(j).start()
            p_copy(j, buf[j], 1).start()
            if C > 2:
                p_copy(j, buf[j], 2).start()

    for j in range(NCH + 1):
        if j < NCH:
            panel_forward(j)
            exchange(j)
        if j > 0:
            assemble(j - 1)

    @pl.when(c == 0)
    def _():
        for j in range(NCH):
            panel_keep(j).wait()

    owner = (c * PB) // pb
    start = lax.rem(c * PB, pb)

    def spread(index, first, out):
        def piece(k, dest):
            return pltpu.make_async_remote_copy(
                src_ref=panel_ref.at[pl.ds(first, PB)],
                dst_ref=out,
                send_sem=ms.at[index, k],
                recv_sem=mr.at[index],
                device_id={"row": dest},
                device_id_type=MESH,
            )

        return piece, pltpu.make_async_copy(panel_ref.at[pl.ds(first, PB)], out, ml.at[index])

    for index, holder, first, out in ((0, owner, start, match_ref), (1, 0, 0, diag_ref)):
        piece, local = spread(index, first, out)

        @pl.when(r == holder)
        def _():
            for o in range(1, R):
                piece(o - 1, lax.rem(r + o, R)).start()
            local.start()

        @pl.when(r != holder)
        def _():
            piece(0, lax.rem(r + 1, R)).wait_recv()

    for index, holder, first, out in ((0, owner, start, match_ref), (1, 0, 0, diag_ref)):
        piece, local = spread(index, first, out)

        @pl.when(r == holder)
        def _():
            for o in range(1, R):
                piece(o - 1, lax.rem(r + o, R)).wait_send()
            local.wait()

    for j in range(NCH):
        out_copy(j).wait()
        for o in range(1, R):
            x_copy(j, o, lax.rem(r + o, R), r).wait_send()

        @pl.loop(1, C)
        def _(d):
            z_copy(j, lax.rem(c + d, C), c).wait_send()

        @pl.when(even)
        def _():
            p_copy(j, panel_ref.at[:, rows(j), :], 1).wait_send()

            @pl.when(c + 2 < C)
            def _():
                p_copy(j, panel_ref.at[:, rows(j), :], 2).wait_send()


def move(order, place, send, front, C, R, nb, cap, pb, cols):
    f32 = jnp.float32
    hbm = pl.BlockSpec(memory_space=pl.ANY)
    smem = pl.BlockSpec(memory_space=pltpu.SMEM)
    dma = pltpu.SemaphoreType.DMA
    big = jax.ShapeDtypeStruct((pb, BLK, cols), f32)
    small = jax.ShapeDtypeStruct((PB, BLK, cols), f32)
    return pl.pallas_call(
        functools.partial(move_kernel, (C, R, nb, cap, pb)),
        out_shape=(big, big, small, small),
        in_specs=[smem, smem, hbm, hbm],
        out_specs=(hbm,) * 4,
        scratch_shapes=[pltpu.VMEM((C * nb, SUB, cols), f32)] * NCH
        + [pltpu.VMEM((R - 1, cap, SUB, cols), f32)] * NCH
        + [pltpu.VMEM((R * cap + 1, SUB, cols), f32)] * NCH
        + [pltpu.VMEM((pb, SUB, cols), f32)] * NCH
        + [
            dma((NCH, C)),
            dma((NCH, C)),
            dma((NCH,)),
            dma((NCH, R - 1)),
            dma((NCH, R)),
            dma((NCH,)),
            dma((NCH,)),
            dma((NCH, 2)),
            dma((NCH,)),
            dma((NCH,)),
            dma((2, R - 1)),
            dma((2,)),
            dma((2,)),
        ],
        compiler_params=pltpu.CompilerParams(
            collective_id=0, has_side_effects=True, vmem_limit_bytes=VMEM_LIMIT
        ),
        cost_estimate=pl.CostEstimate(flops=0, bytes_accessed=64 * 1024 * 1024, transcendentals=0),
    )(order, place, send, front)


STEP = 32


def dot(a, b, ca, cb):
    return lax.dot_general(
        a, b, (((ca,), (cb,)), ((), ())), precision=HI, preferred_element_type=jnp.float32
    )


def factor_kernel(diag_ref, match_ref, factor_ref, gain_ref, work):
    n = PANEL
    block = diag_ref[...]
    row = lax.broadcasted_iota(jnp.int32, (n, n), 0)
    lane = lax.broadcasted_iota(jnp.int32, (n, n), 1)
    work[:, :n] = 0.5 * (block + block.T)
    work[:, n:] = (row == lane).astype(jnp.float32)
    small_row = lax.broadcasted_iota(jnp.int32, (STEP, BLK), 0)
    small_lane = lax.broadcasted_iota(jnp.int32, (STEP, BLK), 1)
    unit = (small_lane == small_row + STEP).astype(jnp.float32)
    for k in range(0, n, STEP):
        tile = work[k:k + STEP, k // BLK * BLK:k // BLK * BLK + BLK]
        tile = pltpu.roll(tile, (BLK - k % BLK) % BLK, 1) if k % BLK else tile
        tile = jnp.where(small_lane < STEP, tile, unit)
        for i in range(STEP):
            scale = lax.rsqrt(tile[i:i + 1, i:i + 1])
            line = tile[i:i + 1, :] * scale
            column = jnp.where(small_row[:, :1] > i, tile[:, i:i + 1] * scale, 0.0)
            tile = jnp.where(small_row == i, line, tile - column * line)
        small_inverse = tile[:, STEP:2 * STEP]
        solved_rows = dot(small_inverse, work[k:k + STEP, :], 1, 0)
        work[k:k + STEP, :] = solved_rows
        if k + STEP < n:
            left = solved_rows[:, :n]
            update = dot(left, solved_rows, 0, 0)
            work[k + STEP:, :] = work[k + STEP:, :] - update[k + STEP:, :]
    upper = jnp.where(lane >= row, work[:, :n], 0.0)
    inverse = jnp.where(lane <= row, work[:, n:], 0.0)
    factor_ref[...] = upper.T
    solved = dot(inverse, match_ref[...], 1, 1)
    both = dot(inverse, solved, 0, 0)
    gain_ref[...] = jnp.where(lax.axis_index("col") == 0, -inverse.T, both)


def factorize(diag, match):
    shape = jax.ShapeDtypeStruct((PANEL, PANEL), jnp.float32)
    return pl.pallas_call(
        factor_kernel,
        out_shape=(shape, shape),
        in_specs=[pl.BlockSpec(memory_space=pltpu.VMEM)] * 2,
        out_specs=(pl.BlockSpec(memory_space=pltpu.VMEM),) * 2,
        scratch_shapes=[pltpu.VMEM((PANEL, 2 * PANEL), jnp.float32)],
        compiler_params=pltpu.CompilerParams(vmem_limit_bytes=32 * 1024 * 1024),
    )(diag, match)


def update_kernel(asm_ref, panel_ref, gain_ref, factor_ref, out_ref):
    first = lax.axis_index("col") == 0
    kept = jnp.where(first, 0.0, asm_ref[...])
    out_ref[...] = kept - dot(panel_ref[...], gain_ref[...], 1, 0)

    @pl.when((lax.axis_index("row") == 0) & (pl.program_id(0) == 0))
    def _():
        out_ref[:PANEL, :] = jnp.where(first, factor_ref[...], asm_ref[:PANEL, :])


def update(asm, panel, gain, factor, tile):
    rows, cols = asm.shape
    line = pl.BlockSpec((tile, cols), lambda i: (i, 0))
    whole = pl.BlockSpec((PANEL, cols), lambda i: (0, 0))
    return pl.pallas_call(
        update_kernel,
        grid=(rows // tile,),
        out_shape=jax.ShapeDtypeStruct((rows, cols), jnp.float32),
        in_specs=[line, line, whole, whole],
        out_specs=line,
        compiler_params=pltpu.CompilerParams(vmem_limit_bytes=32 * 1024 * 1024),
    )(asm, panel, gain, factor)


def body(front_window, children, row_map, col_map):
    R = lax.axis_size("row")
    C = lax.axis_size("col")
    r = lax.axis_index("row")
    rows_here, cols_here = front_window.shape
    child_rows, width = children.shape
    nb = child_rows // BLK
    qb = C * nb
    cap = qb // R
    pb = rows_here // BLK
    i32 = jnp.int32
    sibling = r // (R // 2)
    chosen = lax.dynamic_index_in_dim(col_map, sibling, 0, keepdims=False)
    wb = width // BLK
    ids = jnp.arange(wb, dtype=i32)
    inverse_cols = jnp.sum(jnp.where(chosen[None, :] == ids[:, None], ids[None, :], 0), axis=1)
    maps = row_map.reshape(R, qb)
    owners = maps // pb
    index = jnp.arange(qb, dtype=i32)
    earlier = index[None, :] < index[:, None]
    same = owners[:, :, None] == owners[:, None, :]
    rank = jnp.sum((same & earlier[None]).astype(i32), axis=2)
    mine = lax.dynamic_index_in_dim(owners * cap + rank, r, 0, keepdims=False)
    slots = jnp.arange(R * cap, dtype=i32)
    order = jnp.sum(jnp.where(mine[None, :] == slots[:, None], index[None, :], 0), axis=1)
    slot = (jnp.arange(R, dtype=i32)[:, None] * cap + rank).reshape(row_map.shape)
    wanted = r * pb + jnp.arange(pb, dtype=i32)
    hit = row_map[:, None, :] == wanted[None, :, None]
    found = jnp.sum(jnp.where(hit, slot[:, None, :] + 1, 0), axis=2)
    place = jnp.where(found > 0, found - 1, R * cap).reshape(-1)

    send = pack(children, inverse_cols, C, cols_here).reshape(C, nb, BLK, cols_here)
    asm, panel, match, diag = move(
        order, place, send, front_window.reshape(pb, BLK, cols_here), C, R, nb, cap, pb, cols_here
    )
    factor, gain = factorize(diag.reshape(PANEL, PANEL), match.reshape(PANEL, PANEL))
    return update(
        asm.reshape(rows_here, cols_here), panel.reshape(rows_here, cols_here), gain, factor, 1024
    )


def solution(mesh):
    placed = (
        P(("leaf", "row"), "col"),
        P(("leaf", "row", "col"), None),
        P("leaf", None),
        P("leaf", None),
    )
    return jax.shard_map(
        body, mesh=mesh, in_specs=placed, out_specs=P(("leaf", "row"), "col"), check_vma=False
    )
```

```python
import functools

import jax
import jax.numpy as jnp
from jax import lax
from jax.experimental import pallas as pl
from jax.experimental.pallas import tpu as pltpu
from jax.sharding import PartitionSpec as P

BLK = 128
PANEL = 256
PB = PANEL // BLK
NCH = 8
SUB = BLK // NCH
HI = lax.Precision.HIGHEST
MESH = pl.DeviceIdType.MESH
VMEM_LIMIT = 60 * 1024 * 1024


def pack_kernel(index_ref, child_ref, out_ref):
    out_ref[0] = child_ref[...]


def pack(children, inverse_cols, col_count, cols_here):
    child_rows, width = children.shape
    per = cols_here // BLK
    return pl.pallas_call(
        pack_kernel,
        grid_spec=pltpu.PrefetchScalarGridSpec(
            num_scalar_prefetch=1,
            grid=(width // BLK,),
            in_specs=[pl.BlockSpec((child_rows, BLK), lambda k, idx: (0, idx[k]))],
            out_specs=pl.BlockSpec((1, child_rows, BLK), lambda k, idx: (k // per, 0, k % per)),
        ),
        out_shape=jax.ShapeDtypeStruct((col_count, child_rows, cols_here), jnp.float32),
        compiler_params=pltpu.CompilerParams(vmem_limit_bytes=32 * 1024 * 1024),
    )(inverse_cols, children)


def move_kernel(dims, order_ref, place_ref, send_ref, front_ref, asm_ref, panel_ref, match_ref, diag_ref, *scratch):
    C, R, nb, cap, pb = dims
    zin, xout, xin, buf = (scratch[i * NCH:(i + 1) * NCH] for i in range(4))
    zs, zr, zl, xs, xr, fl, ol, ps, pr, pl_sem, ms, mr, ml = scratch[4 * NCH:]
    c = lax.axis_index("col")
    r = lax.axis_index("row")
    even = lax.rem(c, 2) == 0

    def rows(j):
        return pl.ds(j * SUB, SUB)

    def front_copy(j):
        return pltpu.make_async_copy(front_ref.at[:, rows(j), :], buf[j], fl.at[j])

    def own_copy(j):
        return pltpu.make_async_copy(
            send_ref.at[c, :, rows(j), :], zin[j].at[pl.ds(c * nb, nb)], zl.at[j]
        )

    def z_copy(j, dest, source):
        return pltpu.make_async_remote_copy(
            src_ref=send_ref.at[dest, :, rows(j), :],
            dst_ref=zin[j].at[pl.ds(source * nb, nb)],
            send_sem=zs.at[j, dest],
            recv_sem=zr.at[j, source],
            device_id={"col": dest},
            device_id_type=MESH,
        )

    def x_copy(j, o, dest, source):
        return pltpu.make_async_remote_copy(
            src_ref=xout[j].at[o - 1],
            dst_ref=xin[j].at[pl.ds(source * cap, cap)],
            send_sem=xs.at[j, o - 1],
            recv_sem=xr.at[j, source],
            device_id={"row": dest},
            device_id_type=MESH,
        )

    def p_copy(j, source, hop):
        return pltpu.make_async_remote_copy(
            src_ref=source,
            dst_ref=panel_ref.at[:, rows(j), :],
            send_sem=ps.at[j, hop - 1],
            recv_sem=pr.at[j],
            device_id={"col": lax.rem(c + hop, C)},
            device_id_type=MESH,
        )

    def out_copy(j):
        return pltpu.make_async_copy(buf[j], asm_ref.at[:, rows(j), :], ol.at[j])

    def panel_keep(j):
        return pltpu.make_async_copy(buf[j], panel_ref.at[:, rows(j), :], pl_sem.at[j])

    for j in range(NCH):
        own_copy(j).start()
        front_copy(j).start()
        xin[j][R * cap] = jnp.zeros(xin[j].shape[1:], jnp.float32)

    barrier = pltpu.get_barrier_semaphore()
    for d in range(1, C):
        pl.semaphore_signal(barrier, inc=1, device_id={"col": lax.rem(c + d, C)}, device_id_type=MESH)
    for o in range(1, R):
        pl.semaphore_signal(barrier, inc=1, device_id={"row": lax.rem(r + o, R)}, device_id_type=MESH)
    pl.semaphore_wait(barrier, C + R - 2)

    def z_send(j, chosen):
        @pl.loop(1, C)
        def _(d):
            dest = lax.rem(c + d, C)

            @pl.when((dest != 0) & chosen(dest // 2))
            def _():
                z_copy(j, dest, c).start()

    def above(other):
        return other > c // 2

    def upward(other):
        return other >= c // 2

    def downward(other):
        return other < c // 2

    def not_above(other):
        return other <= c // 2

    @pl.when(jnp.logical_not(even))
    def _():
        for j in range(NCH):
            z_copy(j, 0, c).start()
            z_send(j, upward)
        for j in range(NCH):
            z_send(j, downward)

    def panel_wait(j):
        p_copy(j, panel_ref.at[:, rows(j), :], 1).wait_recv()

    def panel_forward(j):
        panel_wait(j)
        p_copy(j, panel_ref.at[:, rows(j), :], 1).start()

        @pl.when(c + 2 < C)
        def _():
            p_copy(j, panel_ref.at[:, rows(j), :], 2).start()

    def exchange(j):
        own_copy(j).wait()

        @pl.loop(1, C)
        def _(d):
            source = lax.rem(c + d, C)
            z_copy(j, source, source).wait_recv()

        for o in range(1, R):
            dest = lax.rem(r + o, R)

            @pl.loop(0, cap)
            def _(s):
                xout[j][o - 1, s] = zin[j][order_ref[dest * cap + s]]

            x_copy(j, o, dest, r).start()

        @pl.loop(0, cap)
        def _(s):
            xin[j][r * cap + s] = zin[j][order_ref[r * cap + s]]

    def assemble(j):
        front_copy(j).wait()
        for o in range(1, R):
            source = lax.rem(r + o, R)
            x_copy(j, o, source, source).wait_recv()

        @pl.loop(0, pb)
        def _(p):
            buf[j][p] = buf[j][p] + xin[j][place_ref[p]] + xin[j][place_ref[pb + p]]

        out_copy(j).start()

        @pl.when(c == 0)
        def _():
            panel_keep(j).start()
            p_copy(j, buf[j], 1).start()
            if C > 2:
                p_copy(j, buf[j], 2).start()

    @pl.when(even & (c != 0))
    def _():
        for j in range(NCH):
            z_copy(j, 0, c).start()
        for j in range(NCH):
            panel_forward(j)
            z_send(j, not_above)
        for j in range(NCH):
            z_send(j, above)

    for j in range(NCH + 1):
        if j < NCH:
            exchange(j)
        if j > 0:
            assemble(j - 1)

    @pl.when(c == 0)
    def _():
        for j in range(NCH):
            z_send(j, upward)
        for j in range(NCH):
            panel_keep(j).wait()

    @pl.when(jnp.logical_not(even))
    def _():
        for j in range(NCH):
            panel_wait(j)

    owner = (c * PB) // pb
    start = lax.rem(c * PB, pb)

    def spread(index, first, out):
        def piece(k, dest):
            return pltpu.make_async_remote_copy(
                src_ref=panel_ref.at[pl.ds(first, PB)],
                dst_ref=out,
                send_sem=ms.at[index, k],
                recv_sem=mr.at[index],
                device_id={"row": dest},
                device_id_type=MESH,
            )

        return piece, pltpu.make_async_copy(panel_ref.at[pl.ds(first, PB)], out, ml.at[index])

    for index, holder, first, out in ((0, owner, start, match_ref), (1, 0, 0, diag_ref)):
        piece, local = spread(index, first, out)

        @pl.when(r == holder)
        def _():
            for o in range(1, R):
                piece(o - 1, lax.rem(r + o, R)).start()
            local.start()

        @pl.when(r != holder)
        def _():
            piece(0, lax.rem(r + 1, R)).wait_recv()

    for index, holder, first, out in ((0, owner, start, match_ref), (1, 0, 0, diag_ref)):
        piece, local = spread(index, first, out)

        @pl.when(r == holder)
        def _():
            for o in range(1, R):
                piece(o - 1, lax.rem(r + o, R)).wait_send()
            local.wait()

    for j in range(NCH):
        out_copy(j).wait()
        for o in range(1, R):
            x_copy(j, o, lax.rem(r + o, R), r).wait_send()

        @pl.loop(1, C)
        def _(d):
            z_copy(j, lax.rem(c + d, C), c).wait_send()

        @pl.when(even)
        def _():
            p_copy(j, panel_ref.at[:, rows(j), :], 1).wait_send()

            @pl.when(c + 2 < C)
            def _():
                p_copy(j, panel_ref.at[:, rows(j), :], 2).wait_send()


def move(order, place, send, front, C, R, nb, cap, pb, cols):
    f32 = jnp.float32
    hbm = pl.BlockSpec(memory_space=pl.ANY)
    smem = pl.BlockSpec(memory_space=pltpu.SMEM)
    dma = pltpu.SemaphoreType.DMA
    big = jax.ShapeDtypeStruct((pb, BLK, cols), f32)
    small = jax.ShapeDtypeStruct((PB, BLK, cols), f32)
    return pl.pallas_call(
        functools.partial(move_kernel, (C, R, nb, cap, pb)),
        out_shape=(big, big, small, small),
        in_specs=[smem, smem, hbm, hbm],
        out_specs=(hbm,) * 4,
        scratch_shapes=[pltpu.VMEM((C * nb, SUB, cols), f32)] * NCH
        + [pltpu.VMEM((R - 1, cap, SUB, cols), f32)] * NCH
        + [pltpu.VMEM((R * cap + 1, SUB, cols), f32)] * NCH
        + [pltpu.VMEM((pb, SUB, cols), f32)] * NCH
        + [
            dma((NCH, C)),
            dma((NCH, C)),
            dma((NCH,)),
            dma((NCH, R - 1)),
            dma((NCH, R)),
            dma((NCH,)),
            dma((NCH,)),
            dma((NCH, 2)),
            dma((NCH,)),
            dma((NCH,)),
            dma((2, R - 1)),
            dma((2,)),
            dma((2,)),
        ],
        compiler_params=pltpu.CompilerParams(
            collective_id=0, has_side_effects=True, vmem_limit_bytes=VMEM_LIMIT
        ),
        cost_estimate=pl.CostEstimate(flops=0, bytes_accessed=64 * 1024 * 1024, transcendentals=0),
    )(order, place, send, front)


STEP = 32


def dot(a, b, ca, cb):
    return lax.dot_general(
        a, b, (((ca,), (cb,)), ((), ())), precision=HI, preferred_element_type=jnp.float32
    )


def factor_kernel(diag_ref, match_ref, factor_ref, gain_ref, work):
    n = PANEL
    block = diag_ref[...]
    row = lax.broadcasted_iota(jnp.int32, (n, n), 0)
    lane = lax.broadcasted_iota(jnp.int32, (n, n), 1)
    work[:, :n] = 0.5 * (block + block.T)
    work[:, n:] = (row == lane).astype(jnp.float32)
    small_row = lax.broadcasted_iota(jnp.int32, (STEP, BLK), 0)
    small_lane = lax.broadcasted_iota(jnp.int32, (STEP, BLK), 1)
    unit = (small_lane == small_row + STEP).astype(jnp.float32)
    for k in range(0, n, STEP):
        tile = work[k:k + STEP, k // BLK * BLK:k // BLK * BLK + BLK]
        tile = pltpu.roll(tile, (BLK - k % BLK) % BLK, 1) if k % BLK else tile
        tile = jnp.where(small_lane < STEP, tile, unit)
        for i in range(STEP):
            scale = lax.rsqrt(tile[i:i + 1, i:i + 1])
            line = tile[i:i + 1, :] * scale
            column = jnp.where(small_row[:, :1] > i, tile[:, i:i + 1] * scale, 0.0)
            tile = jnp.where(small_row == i, line, tile - column * line)
        small_inverse = tile[:, STEP:2 * STEP]
        solved_rows = dot(small_inverse, work[k:k + STEP, :], 1, 0)
        work[k:k + STEP, :] = solved_rows
        if k + STEP < n:
            left = solved_rows[:, :n]
            update = dot(left, solved_rows, 0, 0)
            work[k + STEP:, :] = work[k + STEP:, :] - update[k + STEP:, :]
    upper = jnp.where(lane >= row, work[:, :n], 0.0)
    inverse = jnp.where(lane <= row, work[:, n:], 0.0)
    factor_ref[...] = upper.T
    solved = dot(inverse, match_ref[...], 1, 1)
    both = dot(inverse, solved, 0, 0)
    gain_ref[...] = jnp.where(lax.axis_index("col") == 0, -inverse.T, both)


def factorize(diag, match):
    shape = jax.ShapeDtypeStruct((PANEL, PANEL), jnp.float32)
    return pl.pallas_call(
        factor_kernel,
        out_shape=(shape, shape),
        in_specs=[pl.BlockSpec(memory_space=pltpu.VMEM)] * 2,
        out_specs=(pl.BlockSpec(memory_space=pltpu.VMEM),) * 2,
        scratch_shapes=[pltpu.VMEM((PANEL, 2 * PANEL), jnp.float32)],
        compiler_params=pltpu.CompilerParams(vmem_limit_bytes=32 * 1024 * 1024),
    )(diag, match)


def update_kernel(asm_ref, panel_ref, gain_ref, factor_ref, out_ref):
    first = lax.axis_index("col") == 0
    kept = jnp.where(first, 0.0, asm_ref[...])
    out_ref[...] = kept - dot(panel_ref[...], gain_ref[...], 1, 0)

    @pl.when((lax.axis_index("row") == 0) & (pl.program_id(0) == 0))
    def _():
        out_ref[:PANEL, :] = jnp.where(first, factor_ref[...], asm_ref[:PANEL, :])


def update(asm, panel, gain, factor, tile):
    rows, cols = asm.shape
    line = pl.BlockSpec((tile, cols), lambda i: (i, 0))
    whole = pl.BlockSpec((PANEL, cols), lambda i: (0, 0))
    return pl.pallas_call(
        update_kernel,
        grid=(rows // tile,),
        out_shape=jax.ShapeDtypeStruct((rows, cols), jnp.float32),
        in_specs=[line, line, whole, whole],
        out_specs=line,
        compiler_params=pltpu.CompilerParams(vmem_limit_bytes=32 * 1024 * 1024),
    )(asm, panel, gain, factor)


def body(front_window, children, row_map, col_map):
    R = lax.axis_size("row")
    C = lax.axis_size("col")
    r = lax.axis_index("row")
    rows_here, cols_here = front_window.shape
    child_rows, width = children.shape
    nb = child_rows // BLK
    qb = C * nb
    cap = qb // R
    pb = rows_here // BLK
    i32 = jnp.int32
    sibling = r // (R // 2)
    chosen = lax.dynamic_index_in_dim(col_map, sibling, 0, keepdims=False)
    wb = width // BLK
    ids = jnp.arange(wb, dtype=i32)
    inverse_cols = jnp.sum(jnp.where(chosen[None, :] == ids[:, None], ids[None, :], 0), axis=1)
    maps = row_map.reshape(R, qb)
    owners = maps // pb
    index = jnp.arange(qb, dtype=i32)
    earlier = index[None, :] < index[:, None]
    same = owners[:, :, None] == owners[:, None, :]
    rank = jnp.sum((same & earlier[None]).astype(i32), axis=2)
    mine = lax.dynamic_index_in_dim(owners * cap + rank, r, 0, keepdims=False)
    slots = jnp.arange(R * cap, dtype=i32)
    order = jnp.sum(jnp.where(mine[None, :] == slots[:, None], index[None, :], 0), axis=1)
    slot = (jnp.arange(R, dtype=i32)[:, None] * cap + rank).reshape(row_map.shape)
    wanted = r * pb + jnp.arange(pb, dtype=i32)
    hit = row_map[:, None, :] == wanted[None, :, None]
    found = jnp.sum(jnp.where(hit, slot[:, None, :] + 1, 0), axis=2)
    place = jnp.where(found > 0, found - 1, R * cap).reshape(-1)

    send = pack(children, inverse_cols, C, cols_here).reshape(C, nb, BLK, cols_here)
    asm, panel, match, diag = move(
        order, place, send, front_window.reshape(pb, BLK, cols_here), C, R, nb, cap, pb, cols_here
    )
    factor, gain = factorize(diag.reshape(PANEL, PANEL), match.reshape(PANEL, PANEL))
    return update(
        asm.reshape(rows_here, cols_here), panel.reshape(rows_here, cols_here), gain, factor, 1024
    )


def solution(mesh):
    placed = (
        P(("leaf", "row"), "col"),
        P(("leaf", "row", "col"), None),
        P("leaf", None),
        P("leaf", None),
    )
    return jax.shard_map(
        body, mesh=mesh, in_specs=placed, out_specs=P(("leaf", "row"), "col"), check_vma=False
    )
```

```python
import functools

import jax
import jax.numpy as jnp
from jax import lax
from jax.experimental import pallas as pl
from jax.experimental.pallas import tpu as pltpu
from jax.sharding import PartitionSpec as P

BLK = 128
PANEL = 256
PB = PANEL // BLK
NCH = 8
SUB = BLK // NCH
HI = lax.Precision.HIGHEST
MESH = pl.DeviceIdType.MESH
VMEM_LIMIT = 60 * 1024 * 1024


def pack_kernel(index_ref, child_ref, out_ref):
    out_ref[0] = child_ref[...]


def pack(children, inverse_cols, col_count, cols_here):
    child_rows, width = children.shape
    per = cols_here // BLK
    return pl.pallas_call(
        pack_kernel,
        grid_spec=pltpu.PrefetchScalarGridSpec(
            num_scalar_prefetch=1,
            grid=(width // BLK,),
            in_specs=[pl.BlockSpec((child_rows, BLK), lambda k, idx: (0, idx[k]))],
            out_specs=pl.BlockSpec((1, child_rows, BLK), lambda k, idx: (k // per, 0, k % per)),
        ),
        out_shape=jax.ShapeDtypeStruct((col_count, child_rows, cols_here), jnp.float32),
        compiler_params=pltpu.CompilerParams(vmem_limit_bytes=VMEM_LIMIT),
    )(inverse_cols, children)


def move_kernel(dims, order_ref, place_ref, send_ref, front_ref, asm_ref, panel_ref, match_ref, diag_ref, *scratch):
    C, R, nb, cap, pb = dims
    zin, xout, xin, buf = (scratch[i * NCH:(i + 1) * NCH] for i in range(4))
    zs, zr, zl, xs, xr, fl, ol, ps, pr, pl_sem, ms, mr, ml = scratch[4 * NCH:]
    c = lax.axis_index("col")
    r = lax.axis_index("row")
    even = lax.rem(c, 2) == 0

    def rows(j):
        return pl.ds(j * SUB, SUB)

    def front_copy(j):
        return pltpu.make_async_copy(front_ref.at[:, rows(j), :], buf[j], fl.at[j])

    def own_copy(j):
        return pltpu.make_async_copy(
            send_ref.at[c, :, rows(j), :], zin[j].at[pl.ds(c * nb, nb)], zl.at[j]
        )

    def z_copy(j, dest, source):
        return pltpu.make_async_remote_copy(
            src_ref=send_ref.at[dest, :, rows(j), :],
            dst_ref=zin[j].at[pl.ds(source * nb, nb)],
            send_sem=zs.at[j, dest],
            recv_sem=zr.at[j, source],
            device_id={"col": dest},
            device_id_type=MESH,
        )

    def x_copy(j, o, dest, source):
        return pltpu.make_async_remote_copy(
            src_ref=xout[j].at[o - 1],
            dst_ref=xin[j].at[pl.ds(source * cap, cap)],
            send_sem=xs.at[j, o - 1],
            recv_sem=xr.at[j, source],
            device_id={"row": dest},
            device_id_type=MESH,
        )

    def p_copy(j, source, hop):
        return pltpu.make_async_remote_copy(
            src_ref=source,
            dst_ref=panel_ref.at[:, rows(j), :],
            send_sem=ps.at[j, hop - 1],
            recv_sem=pr.at[j],
            device_id={"col": lax.rem(c + hop, C)},
            device_id_type=MESH,
        )

    def out_copy(j):
        return pltpu.make_async_copy(buf[j], asm_ref.at[:, rows(j), :], ol.at[j])

    def panel_keep(j):
        return pltpu.make_async_copy(buf[j], panel_ref.at[:, rows(j), :], pl_sem.at[j])

    for j in range(NCH):
        own_copy(j).start()
        front_copy(j).start()
        xin[j][R * cap] = jnp.zeros(xin[j].shape[1:], jnp.float32)

    barrier = pltpu.get_barrier_semaphore()
    for d in range(1, C):
        pl.semaphore_signal(barrier, inc=1, device_id={"col": lax.rem(c + d, C)}, device_id_type=MESH)
    for o in range(1, R):
        pl.semaphore_signal(barrier, inc=1, device_id={"row": lax.rem(r + o, R)}, device_id_type=MESH)
    pl.semaphore_wait(barrier, C + R - 2)

    for j in range(NCH):

        @pl.when(c != 0)
        def _():
            for t in range(2 * j, min(2 * j + 2, NCH)):
                z_copy(t, 0, c).start()

        @pl.loop(1, C)
        def _(d):
            dest = lax.rem(c + d, C)

            @pl.when(dest != 0)
            def _():
                z_copy(j, dest, c).start()

    def panel_forward(j):
        @pl.when(c != 0)
        def _():
            p_copy(j, panel_ref.at[:, rows(j), :], 1).wait_recv()

            @pl.when(even)
            def _():
                p_copy(j, panel_ref.at[:, rows(j), :], 1).start()

                @pl.when(c + 2 < C)
                def _():
                    p_copy(j, panel_ref.at[:, rows(j), :], 2).start()

    def exchange(j):
        own_copy(j).wait()

        @pl.loop(1, C)
        def _(d):
            source = lax.rem(c + d, C)
            z_copy(j, source, source).wait_recv()

        for o in range(1, R):
            dest = lax.rem(r + o, R)

            @pl.loop(0, cap)
            def _(s):
                xout[j][o - 1, s] = zin[j][order_ref[dest * cap + s]]

            x_copy(j, o, dest, r).start()

        @pl.loop(0, cap)
        def _(s):
            xin[j][r * cap + s] = zin[j][order_ref[r * cap + s]]

    def assemble(j):
        front_copy(j).wait()
        for o in range(1, R):
            source = lax.rem(r + o, R)
            x_copy(j, o, source, source).wait_recv()

        @pl.loop(0, pb)
        def _(p):
            buf[j][p] = buf[j][p] + xin[j][place_ref[p]] + xin[j][place_ref[pb + p]]

        out_copy(j).start()

        @pl.when(c == 0)
        def _():
            panel_keep(j).start()
            p_copy(j, buf[j], 1).start()
            if C > 2:
                p_copy(j, buf[j], 2).start()

    for j in range(NCH + 1):
        if j < NCH:
            exchange(j)
        if j > 0:
            assemble(j - 1)

    for j in range(NCH):
        panel_forward(j)

    @pl.when(c == 0)
    def _():
        for j in range(NCH):
            panel_keep(j).wait()

    owner = (c * PB) // pb
    start = lax.rem(c * PB, pb)

    def spread(index, first, out):
        def piece(k, dest):
            return pltpu.make_async_remote_copy(
                src_ref=panel_ref.at[pl.ds(first, PB)],
                dst_ref=out,
                send_sem=ms.at[index, k],
                recv_sem=mr.at[index],
                device_id={"row": dest},
                device_id_type=MESH,
            )

        return piece, pltpu.make_async_copy(panel_ref.at[pl.ds(first, PB)], out, ml.at[index])

    for index, holder, first, out in ((0, owner, start, match_ref), (1, 0, 0, diag_ref)):
        piece, local = spread(index, first, out)

        @pl.when(r == holder)
        def _():
            for o in range(1, R):
                piece(o - 1, lax.rem(r + o, R)).start()
            local.start()

        @pl.when(r != holder)
        def _():
            piece(0, lax.rem(r + 1, R)).wait_recv()

    for index, holder, first, out in ((0, owner, start, match_ref), (1, 0, 0, diag_ref)):
        piece, local = spread(index, first, out)

        @pl.when(r == holder)
        def _():
            for o in range(1, R):
                piece(o - 1, lax.rem(r + o, R)).wait_send()
            local.wait()

    for j in range(NCH):
        out_copy(j).wait()
        for o in range(1, R):
            x_copy(j, o, lax.rem(r + o, R), r).wait_send()

        @pl.loop(1, C)
        def _(d):
            z_copy(j, lax.rem(c + d, C), c).wait_send()

        @pl.when(even)
        def _():
            p_copy(j, panel_ref.at[:, rows(j), :], 1).wait_send()

            @pl.when(c + 2 < C)
            def _():
                p_copy(j, panel_ref.at[:, rows(j), :], 2).wait_send()


def move(order, place, send, front, C, R, nb, cap, pb, cols):
    f32 = jnp.float32
    hbm = pl.BlockSpec(memory_space=pl.ANY)
    smem = pl.BlockSpec(memory_space=pltpu.SMEM)
    dma = pltpu.SemaphoreType.DMA
    big = jax.ShapeDtypeStruct((pb, BLK, cols), f32)
    small = jax.ShapeDtypeStruct((PB, BLK, cols), f32)
    return pl.pallas_call(
        functools.partial(move_kernel, (C, R, nb, cap, pb)),
        out_shape=(big, big, small, small),
        in_specs=[smem, smem, hbm, hbm],
        out_specs=(hbm,) * 4,
        scratch_shapes=[pltpu.VMEM((C * nb, SUB, cols), f32)] * NCH
        + [pltpu.VMEM((R - 1, cap, SUB, cols), f32)] * NCH
        + [pltpu.VMEM((R * cap + 1, SUB, cols), f32)] * NCH
        + [pltpu.VMEM((pb, SUB, cols), f32)] * NCH
        + [
            dma((NCH, C)),
            dma((NCH, C)),
            dma((NCH,)),
            dma((NCH, R - 1)),
            dma((NCH, R)),
            dma((NCH,)),
            dma((NCH,)),
            dma((NCH, 2)),
            dma((NCH,)),
            dma((NCH,)),
            dma((2, R - 1)),
            dma((2,)),
            dma((2,)),
        ],
        compiler_params=pltpu.CompilerParams(
            collective_id=0, has_side_effects=True, vmem_limit_bytes=VMEM_LIMIT
        ),
        cost_estimate=pl.CostEstimate(flops=0, bytes_accessed=64 * 1024 * 1024, transcendentals=0),
    )(order, place, send, front)


STEP = 32


def dot(a, b, ca, cb):
    return lax.dot_general(
        a, b, (((ca,), (cb,)), ((), ())), precision=HI, preferred_element_type=jnp.float32
    )


def factor_kernel(diag_ref, match_ref, factor_ref, gain_ref, work):
    n = PANEL
    block = diag_ref[...]
    row = lax.broadcasted_iota(jnp.int32, (n, n), 0)
    lane = lax.broadcasted_iota(jnp.int32, (n, n), 1)
    work[:, :n] = 0.5 * (block + block.T)
    work[:, n:] = (row == lane).astype(jnp.float32)
    small_row = lax.broadcasted_iota(jnp.int32, (STEP, BLK), 0)
    small_lane = lax.broadcasted_iota(jnp.int32, (STEP, BLK), 1)
    unit = (small_lane == small_row + STEP).astype(jnp.float32)
    for k in range(0, n, STEP):
        tile = work[k:k + STEP, k // BLK * BLK:k // BLK * BLK + BLK]
        tile = pltpu.roll(tile, (BLK - k % BLK) % BLK, 1) if k % BLK else tile
        tile = jnp.where(small_lane < STEP, tile, unit)
        for i in range(STEP):
            scale = lax.rsqrt(tile[i:i + 1, i:i + 1])
            line = tile[i:i + 1, :] * scale
            column = jnp.where(small_row[:, :1] > i, tile[:, i:i + 1] * scale, 0.0)
            tile = jnp.where(small_row == i, line, tile - column * line)
        small_inverse = tile[:, STEP:2 * STEP]
        solved_rows = dot(small_inverse, work[k:k + STEP, :], 1, 0)
        work[k:k + STEP, :] = solved_rows
        if k + STEP < n:
            left = solved_rows[:, :n]
            update = dot(left, solved_rows, 0, 0)
            work[k + STEP:, :] = work[k + STEP:, :] - update[k + STEP:, :]
    upper = jnp.where(lane >= row, work[:, :n], 0.0)
    inverse = jnp.where(lane <= row, work[:, n:], 0.0)
    factor_ref[...] = upper.T
    solved = dot(inverse, match_ref[...], 1, 1)
    both = dot(inverse, solved, 0, 0)
    gain_ref[...] = jnp.where(lax.axis_index("col") == 0, -inverse.T, both)


def factorize(diag, match):
    shape = jax.ShapeDtypeStruct((PANEL, PANEL), jnp.float32)
    return pl.pallas_call(
        factor_kernel,
        out_shape=(shape, shape),
        in_specs=[pl.BlockSpec(memory_space=pltpu.VMEM)] * 2,
        out_specs=(pl.BlockSpec(memory_space=pltpu.VMEM),) * 2,
        scratch_shapes=[pltpu.VMEM((PANEL, 2 * PANEL), jnp.float32)],
        compiler_params=pltpu.CompilerParams(vmem_limit_bytes=VMEM_LIMIT),
    )(diag, match)


def update_kernel(asm_ref, panel_ref, gain_ref, factor_ref, out_ref):
    first = lax.axis_index("col") == 0
    kept = jnp.where(first, 0.0, asm_ref[...])
    out_ref[...] = kept - dot(panel_ref[...], gain_ref[...], 1, 0)

    @pl.when((lax.axis_index("row") == 0) & (pl.program_id(0) == 0))
    def _():
        out_ref[:PANEL, :] = jnp.where(first, factor_ref[...], asm_ref[:PANEL, :])


def update(asm, panel, gain, factor, tile):
    rows, cols = asm.shape
    line = pl.BlockSpec((tile, cols), lambda i: (i, 0))
    whole = pl.BlockSpec((PANEL, cols), lambda i: (0, 0))
    return pl.pallas_call(
        update_kernel,
        grid=(rows // tile,),
        out_shape=jax.ShapeDtypeStruct((rows, cols), jnp.float32),
        in_specs=[line, line, whole, whole],
        out_specs=line,
        compiler_params=pltpu.CompilerParams(vmem_limit_bytes=VMEM_LIMIT),
    )(asm, panel, gain, factor)


def body(front_window, children, row_map, col_map):
    R = lax.axis_size("row")
    C = lax.axis_size("col")
    r = lax.axis_index("row")
    rows_here, cols_here = front_window.shape
    child_rows, width = children.shape
    nb = child_rows // BLK
    qb = C * nb
    cap = qb // R
    pb = rows_here // BLK
    i32 = jnp.int32
    sibling = r // (R // 2)
    chosen = lax.dynamic_index_in_dim(col_map, sibling, 0, keepdims=False)
    wb = width // BLK
    ids = jnp.arange(wb, dtype=i32)
    inverse_cols = jnp.sum(jnp.where(chosen[None, :] == ids[:, None], ids[None, :], 0), axis=1)
    maps = row_map.reshape(R, qb)
    owners = maps // pb
    index = jnp.arange(qb, dtype=i32)
    earlier = index[None, :] < index[:, None]
    same = owners[:, :, None] == owners[:, None, :]
    rank = jnp.sum((same & earlier[None]).astype(i32), axis=2)
    mine = lax.dynamic_index_in_dim(owners * cap + rank, r, 0, keepdims=False)
    slots = jnp.arange(R * cap, dtype=i32)
    order = jnp.sum(jnp.where(mine[None, :] == slots[:, None], index[None, :], 0), axis=1)
    slot = (jnp.arange(R, dtype=i32)[:, None] * cap + rank).reshape(row_map.shape)
    wanted = r * pb + jnp.arange(pb, dtype=i32)
    hit = row_map[:, None, :] == wanted[None, :, None]
    found = jnp.sum(jnp.where(hit, slot[:, None, :] + 1, 0), axis=2)
    place = jnp.where(found > 0, found - 1, R * cap).reshape(-1)

    send = pack(children, inverse_cols, C, cols_here).reshape(C, nb, BLK, cols_here)
    asm, panel, match, diag = move(
        order, place, send, front_window.reshape(pb, BLK, cols_here), C, R, nb, cap, pb, cols_here
    )
    factor, gain = factorize(diag.reshape(PANEL, PANEL), match.reshape(PANEL, PANEL))
    return update(
        asm.reshape(rows_here, cols_here), panel.reshape(rows_here, cols_here), gain, factor, 1024
    )


def solution(mesh):
    placed = (
        P(("leaf", "row"), "col"),
        P(("leaf", "row", "col"), None),
        P("leaf", None),
        P("leaf", None),
    )
    return jax.shard_map(
        body, mesh=mesh, in_specs=placed, out_specs=P(("leaf", "row"), "col"), check_vma=False
    )
```

```python
import functools

import jax
import jax.numpy as jnp
from jax import lax
from jax.experimental import pallas as pl
from jax.experimental.pallas import tpu as pltpu
from jax.sharding import PartitionSpec as P

BLK = 128
PANEL = 256
PB = PANEL // BLK
NCH = 8
SUB = BLK // NCH
HI = lax.Precision.HIGHEST
MESH = pl.DeviceIdType.MESH
VMEM_LIMIT = 60 * 1024 * 1024


def pack_kernel(index_ref, child_ref, out_ref):
    out_ref[0] = child_ref[...]


def pack(children, inverse_cols, col_count, cols_here):
    child_rows, width = children.shape
    per = cols_here // BLK
    return pl.pallas_call(
        pack_kernel,
        grid_spec=pltpu.PrefetchScalarGridSpec(
            num_scalar_prefetch=1,
            grid=(width // BLK,),
            in_specs=[pl.BlockSpec((child_rows, BLK), lambda k, idx: (0, idx[k]))],
            out_specs=pl.BlockSpec((1, child_rows, BLK), lambda k, idx: (k // per, 0, k % per)),
        ),
        out_shape=jax.ShapeDtypeStruct((col_count, child_rows, cols_here), jnp.float32),
        compiler_params=pltpu.CompilerParams(vmem_limit_bytes=VMEM_LIMIT),
    )(inverse_cols, children)


def move_kernel(dims, order_ref, place_ref, send_ref, front_ref, asm_ref, panel_ref, match_ref, diag_ref, *scratch):
    C, R, nb, cap, pb = dims
    zin, xout, xin, buf = (scratch[i * NCH:(i + 1) * NCH] for i in range(4))
    zs, zr, zl, xs, xr, fl, ol, ps, pr, pl_sem, ms, mr, ml = scratch[4 * NCH:]
    c = lax.axis_index("col")
    r = lax.axis_index("row")
    even = lax.rem(c, 2) == 0
    relays = even & (c != 0) & (c + 2 < C)

    def rows(j):
        return pl.ds(j * SUB, SUB)

    def front_copy(j):
        return pltpu.make_async_copy(front_ref.at[:, rows(j), :], buf[j], fl.at[j])

    def own_copy(j):
        return pltpu.make_async_copy(
            send_ref.at[c, :, rows(j), :], zin[j].at[pl.ds(c * nb, nb)], zl.at[j]
        )

    def z_copy(j, dest, source):
        return pltpu.make_async_remote_copy(
            src_ref=send_ref.at[dest, :, rows(j), :],
            dst_ref=zin[j].at[pl.ds(source * nb, nb)],
            send_sem=zs.at[j, dest],
            recv_sem=zr.at[j, source],
            device_id={"col": dest},
            device_id_type=MESH,
        )

    def x_copy(j, o, dest, source):
        return pltpu.make_async_remote_copy(
            src_ref=xout[j].at[o - 1],
            dst_ref=xin[j].at[pl.ds(source * cap, cap)],
            send_sem=xs.at[j, o - 1],
            recv_sem=xr.at[j, source],
            device_id={"row": dest},
            device_id_type=MESH,
        )

    def p_copy(j, source, hop):
        return pltpu.make_async_remote_copy(
            src_ref=source,
            dst_ref=panel_ref.at[:, rows(j), :],
            send_sem=ps.at[j, hop - 1],
            recv_sem=pr.at[j],
            device_id={"col": lax.rem(c + hop, C)},
            device_id_type=MESH,
        )

    def out_copy(j):
        return pltpu.make_async_copy(buf[j], asm_ref.at[:, rows(j), :], ol.at[j])

    def panel_keep(j):
        return pltpu.make_async_copy(buf[j], panel_ref.at[:, rows(j), :], pl_sem.at[j])

    for j in range(NCH):
        own_copy(j).start()
        front_copy(j).start()
        xin[j][R * cap] = jnp.zeros(xin[j].shape[1:], jnp.float32)

    barrier = pltpu.get_barrier_semaphore()
    for d in range(1, C):
        pl.semaphore_signal(barrier, inc=1, device_id={"col": lax.rem(c + d, C)}, device_id_type=MESH)
    for o in range(1, R):
        pl.semaphore_signal(barrier, inc=1, device_id={"row": lax.rem(r + o, R)}, device_id_type=MESH)
    pl.semaphore_wait(barrier, C + R - 2)

    for j in range(NCH):

        @pl.when(c != 0)
        def _():
            for t in range(2 * j, min(2 * j + 2, NCH)):
                z_copy(t, 0, c).start()

        @pl.loop(1, C)
        def _(d):
            dest = lax.rem(c + d, C)

            @pl.when(dest != 0)
            def _():
                z_copy(j, dest, c).start()

    def panel_forward(j):
        @pl.when(c != 0)
        def _():
            p_copy(j, panel_ref.at[:, rows(j), :], 1).wait_recv()

            @pl.when(even)
            def _():
                p_copy(j, panel_ref.at[:, rows(j), :], 1).start()

                @pl.when(c + 2 < C)
                def _():
                    p_copy(j, panel_ref.at[:, rows(j), :], 2).start()

    def exchange(j):
        own_copy(j).wait()

        @pl.loop(1, C)
        def _(d):
            source = lax.rem(c + d, C)
            z_copy(j, source, source).wait_recv()

        for o in range(1, R):
            dest = lax.rem(r + o, R)

            @pl.loop(0, cap)
            def _(s):
                xout[j][o - 1, s] = zin[j][order_ref[dest * cap + s]]

            x_copy(j, o, dest, r).start()

        @pl.loop(0, cap)
        def _(s):
            xin[j][r * cap + s] = zin[j][order_ref[r * cap + s]]

    def assemble(j):
        front_copy(j).wait()
        for o in range(1, R):
            source = lax.rem(r + o, R)
            x_copy(j, o, source, source).wait_recv()

        @pl.loop(0, pb)
        def _(p):
            buf[j][p] = buf[j][p] + xin[j][place_ref[p]] + xin[j][place_ref[pb + p]]

        out_copy(j).start()

        @pl.when(c == 0)
        def _():
            panel_keep(j).start()
            p_copy(j, buf[j], 1).start()
            if C > 2:
                p_copy(j, buf[j], 2).start()

    for j in range(NCH + 1):
        if j < NCH:
            exchange(j)
        if j > 0:
            assemble(j - 1)
        if NCH - 3 <= j < NCH:

            @pl.when(relays)
            def _():
                for t in range(2 * (j - NCH + 3), 2 * (j - NCH + 3) + 2):
                    panel_forward(t)

    for j in range(NCH):
        if j < 6:

            @pl.when(jnp.logical_not(relays))
            def _():
                panel_forward(j)
        else:
            panel_forward(j)

    @pl.when(c == 0)
    def _():
        for j in range(NCH):
            panel_keep(j).wait()

    owner = (c * PB) // pb
    start = lax.rem(c * PB, pb)

    def spread(index, first, out):
        def piece(k, dest):
            return pltpu.make_async_remote_copy(
                src_ref=panel_ref.at[pl.ds(first, PB)],
                dst_ref=out,
                send_sem=ms.at[index, k],
                recv_sem=mr.at[index],
                device_id={"row": dest},
                device_id_type=MESH,
            )

        return piece, pltpu.make_async_copy(panel_ref.at[pl.ds(first, PB)], out, ml.at[index])

    for index, holder, first, out in ((0, owner, start, match_ref), (1, 0, 0, diag_ref)):
        piece, local = spread(index, first, out)

        @pl.when(r == holder)
        def _():
            for o in range(1, R):
                piece(o - 1, lax.rem(r + o, R)).start()
            local.start()

        @pl.when(r != holder)
        def _():
            piece(0, lax.rem(r + 1, R)).wait_recv()

    for index, holder, first, out in ((0, owner, start, match_ref), (1, 0, 0, diag_ref)):
        piece, local = spread(index, first, out)

        @pl.when(r == holder)
        def _():
            for o in range(1, R):
                piece(o - 1, lax.rem(r + o, R)).wait_send()
            local.wait()

    for j in range(NCH):
        out_copy(j).wait()
        for o in range(1, R):
            x_copy(j, o, lax.rem(r + o, R), r).wait_send()

        @pl.loop(1, C)
        def _(d):
            z_copy(j, lax.rem(c + d, C), c).wait_send()

        @pl.when(even)
        def _():
            p_copy(j, panel_ref.at[:, rows(j), :], 1).wait_send()

            @pl.when(c + 2 < C)
            def _():
                p_copy(j, panel_ref.at[:, rows(j), :], 2).wait_send()


def move(order, place, send, front, C, R, nb, cap, pb, cols):
    f32 = jnp.float32
    hbm = pl.BlockSpec(memory_space=pl.ANY)
    smem = pl.BlockSpec(memory_space=pltpu.SMEM)
    dma = pltpu.SemaphoreType.DMA
    big = jax.ShapeDtypeStruct((pb, BLK, cols), f32)
    small = jax.ShapeDtypeStruct((PB, BLK, cols), f32)
    return pl.pallas_call(
        functools.partial(move_kernel, (C, R, nb, cap, pb)),
        out_shape=(big, big, small, small),
        in_specs=[smem, smem, hbm, hbm],
        out_specs=(hbm,) * 4,
        scratch_shapes=[pltpu.VMEM((C * nb, SUB, cols), f32)] * NCH
        + [pltpu.VMEM((R - 1, cap, SUB, cols), f32)] * NCH
        + [pltpu.VMEM((R * cap + 1, SUB, cols), f32)] * NCH
        + [pltpu.VMEM((pb, SUB, cols), f32)] * NCH
        + [
            dma((NCH, C)),
            dma((NCH, C)),
            dma((NCH,)),
            dma((NCH, R - 1)),
            dma((NCH, R)),
            dma((NCH,)),
            dma((NCH,)),
            dma((NCH, 2)),
            dma((NCH,)),
            dma((NCH,)),
            dma((2, R - 1)),
            dma((2,)),
            dma((2,)),
        ],
        compiler_params=pltpu.CompilerParams(
            collective_id=0, has_side_effects=True, vmem_limit_bytes=VMEM_LIMIT
        ),
        cost_estimate=pl.CostEstimate(flops=0, bytes_accessed=64 * 1024 * 1024, transcendentals=0),
    )(order, place, send, front)


STEP = 32


def dot(a, b, ca, cb):
    return lax.dot_general(
        a, b, (((ca,), (cb,)), ((), ())), precision=HI, preferred_element_type=jnp.float32
    )


def factor_kernel(diag_ref, match_ref, factor_ref, gain_ref, work):
    n = PANEL
    block = diag_ref[...]
    row = lax.broadcasted_iota(jnp.int32, (n, n), 0)
    lane = lax.broadcasted_iota(jnp.int32, (n, n), 1)
    work[:, :n] = 0.5 * (block + block.T)
    work[:, n:] = (row == lane).astype(jnp.float32)
    small_row = lax.broadcasted_iota(jnp.int32, (STEP, BLK), 0)
    small_lane = lax.broadcasted_iota(jnp.int32, (STEP, BLK), 1)
    unit = (small_lane == small_row + STEP).astype(jnp.float32)
    for k in range(0, n, STEP):
        tile = work[k:k + STEP, k // BLK * BLK:k // BLK * BLK + BLK]
        tile = pltpu.roll(tile, (BLK - k % BLK) % BLK, 1) if k % BLK else tile
        tile = jnp.where(small_lane < STEP, tile, unit)
        for i in range(STEP):
            scale = lax.rsqrt(tile[i:i + 1, i:i + 1])
            line = tile[i:i + 1, :] * scale
            column = jnp.where(small_row[:, :1] > i, tile[:, i:i + 1] * scale, 0.0)
            tile = jnp.where(small_row == i, line, tile - column * line)
        small_inverse = tile[:, STEP:2 * STEP]
        solved_rows = dot(small_inverse, work[k:k + STEP, :], 1, 0)
        work[k:k + STEP, :] = solved_rows
        if k + STEP < n:
            left = solved_rows[:, :n]
            update = dot(left, solved_rows, 0, 0)
            work[k + STEP:, :] = work[k + STEP:, :] - update[k + STEP:, :]
    upper = jnp.where(lane >= row, work[:, :n], 0.0)
    inverse = jnp.where(lane <= row, work[:, n:], 0.0)
    factor_ref[...] = upper.T
    solved = dot(inverse, match_ref[...], 1, 1)
    both = dot(inverse, solved, 0, 0)
    gain_ref[...] = jnp.where(lax.axis_index("col") == 0, -inverse.T, both)


def factorize(diag, match):
    shape = jax.ShapeDtypeStruct((PANEL, PANEL), jnp.float32)
    return pl.pallas_call(
        factor_kernel,
        out_shape=(shape, shape),
        in_specs=[pl.BlockSpec(memory_space=pltpu.VMEM)] * 2,
        out_specs=(pl.BlockSpec(memory_space=pltpu.VMEM),) * 2,
        scratch_shapes=[pltpu.VMEM((PANEL, 2 * PANEL), jnp.float32)],
        compiler_params=pltpu.CompilerParams(vmem_limit_bytes=VMEM_LIMIT),
    )(diag, match)


def update_kernel(asm_ref, panel_ref, gain_ref, factor_ref, out_ref):
    first = lax.axis_index("col") == 0
    kept = jnp.where(first, 0.0, asm_ref[...])
    out_ref[...] = kept - dot(panel_ref[...], gain_ref[...], 1, 0)

    @pl.when((lax.axis_index("row") == 0) & (pl.program_id(0) == 0))
    def _():
        out_ref[:PANEL, :] = jnp.where(first, factor_ref[...], asm_ref[:PANEL, :])


def update(asm, panel, gain, factor, tile):
    rows, cols = asm.shape
    line = pl.BlockSpec((tile, cols), lambda i: (i, 0))
    whole = pl.BlockSpec((PANEL, cols), lambda i: (0, 0))
    return pl.pallas_call(
        update_kernel,
        grid=(rows // tile,),
        out_shape=jax.ShapeDtypeStruct((rows, cols), jnp.float32),
        in_specs=[line, line, whole, whole],
        out_specs=line,
        compiler_params=pltpu.CompilerParams(vmem_limit_bytes=VMEM_LIMIT),
    )(asm, panel, gain, factor)


def body(front_window, children, row_map, col_map):
    R = lax.axis_size("row")
    C = lax.axis_size("col")
    r = lax.axis_index("row")
    rows_here, cols_here = front_window.shape
    child_rows, width = children.shape
    nb = child_rows // BLK
    qb = C * nb
    cap = qb // R
    pb = rows_here // BLK
    i32 = jnp.int32
    sibling = r // (R // 2)
    chosen = lax.dynamic_index_in_dim(col_map, sibling, 0, keepdims=False)
    wb = width // BLK
    ids = jnp.arange(wb, dtype=i32)
    inverse_cols = jnp.sum(jnp.where(chosen[None, :] == ids[:, None], ids[None, :], 0), axis=1)
    maps = row_map.reshape(R, qb)
    owners = maps // pb
    index = jnp.arange(qb, dtype=i32)
    earlier = index[None, :] < index[:, None]
    same = owners[:, :, None] == owners[:, None, :]
    rank = jnp.sum((same & earlier[None]).astype(i32), axis=2)
    mine = lax.dynamic_index_in_dim(owners * cap + rank, r, 0, keepdims=False)
    slots = jnp.arange(R * cap, dtype=i32)
    order = jnp.sum(jnp.where(mine[None, :] == slots[:, None], index[None, :], 0), axis=1)
    slot = (jnp.arange(R, dtype=i32)[:, None] * cap + rank).reshape(row_map.shape)
    wanted = r * pb + jnp.arange(pb, dtype=i32)
    hit = row_map[:, None, :] == wanted[None, :, None]
    found = jnp.sum(jnp.where(hit, slot[:, None, :] + 1, 0), axis=2)
    place = jnp.where(found > 0, found - 1, R * cap).reshape(-1)

    send = pack(children, inverse_cols, C, cols_here).reshape(C, nb, BLK, cols_here)
    asm, panel, match, diag = move(
        order, place, send, front_window.reshape(pb, BLK, cols_here), C, R, nb, cap, pb, cols_here
    )
    factor, gain = factorize(diag.reshape(PANEL, PANEL), match.reshape(PANEL, PANEL))
    return update(
        asm.reshape(rows_here, cols_here), panel.reshape(rows_here, cols_here), gain, factor, 1024
    )


def solution(mesh):
    placed = (
        P(("leaf", "row"), "col"),
        P(("leaf", "row", "col"), None),
        P("leaf", None),
        P("leaf", None),
    )
    return jax.shard_map(
        body, mesh=mesh, in_specs=placed, out_specs=P(("leaf", "row"), "col"), check_vma=False
    )
```
